256 devices in a mesh: ctx: 64 (over x, z, core), head: 4 (over y).
Axes of the slice: x: 4, y: 4, z: 8, core: 2. Of those that a mesh axis runs over, the one named last changes fastest.
Arguments:
- queries: bfloat16 [12288, 512], P('ctx', 'head'), may hold values from -32 to 32, as said below
- key_rows: bfloat16 [12288, 512], P('ctx', 'head'), may hold values from -12 to 12
- value_rows: bfloat16 [12288, 512], P('ctx', 'head'), may hold values from -5 to 5
- out_grads: bfloat16 [12288, 512], P('ctx', 'head'), may hold values from -5 to 5
- query_proj: bfloat16 [5120, 512], P(None, 'head'), may hold values from -0.25 to 0.25
- key_proj: bfloat16 [5120, 512], P(None, 'head'), may hold values from -0.25 to 0.25
- value_proj: bfloat16 [5120, 512], P(None, 'head'), may hold values from -0.25 to 0.25
Outputs:
- d_input: bfloat16 [12288, 5120], P('ctx', 'head')
The draws below stay inside these ranges and needn't reach their ends.
Inputs may be any that keep to these rules, and one draw needn't show every extreme that they name: queries of one head times its keys stay of order one on most rows; some rows may be much larger.
All inputs are finite; a program needn't handle non-finite values.
Results may differ from the reference program's by a relative error of at most 0.0063.
Values may be sent and summed in bfloat16 or wider, within the bound.
No kernel may reach another device: no remote copies, remote signals or barrier semaphores. Data moves between devices by JAX's collectives and lax.ppermute only.
A program may use at most 64 MiB of HBM per device.

```python
import math
import jax
import jax.numpy as jnp
from jax import lax

D = 5120
HEAD_DIM = 128
TOK_DEV = 192
HEADS = 4
TOKENS = 12288


def shared_rows(key):
    base = jnp.clip(jax.random.normal(key, (TOKENS, HEADS * HEAD_DIM), jnp.float32), -4.0, 4.0)
    return base


def draw_queries(key, part):
    base = shared_rows(key)
    key = jax.random.fold_in(key, 11)
    result = 2.5 * jnp.clip(jax.random.normal(key, base.shape, jnp.float32), -4.0, 4.0)
    return result.astype(jnp.bfloat16)


def draw_key_rows(key, part):
    base = shared_rows(key)
    key = jax.random.fold_in(key, 12)
    result = jnp.clip(jax.random.normal(key, base.shape, jnp.float32), -4.0, 4.0)
    return result.astype(jnp.bfloat16)


def shard_levels(own_key, extent, split, smallest, largest):
    gain, own = 1.0, jax.random.fold_in(own_key, 6)
    for dim, blocks in split:
        steps = jnp.exp(jax.random.uniform(jax.random.fold_in(own, dim), (blocks,), jnp.float32, smallest / len(split), largest / len(split)))
        gain = gain * jnp.repeat(steps, extent[dim] // blocks).reshape([-1 if axis == dim else 1 for axis in range(len(extent))])
    return gain


def normal_values(own_key, shape, scale, bound, cuts=(), kind=jnp.bfloat16):
    level = shard_levels(own_key, shape, cuts, -0.22, 0.18) if cuts else 1.0
    values = jax.random.normal(own_key, shape, jnp.float32) * scale * level
    return jnp.minimum(jnp.maximum(values, -bound), bound).astype(kind)


def setup_inputs(seed: int = 0) -> dict:
    streams_of = jax.random.split(jax.random.key(seed), 8)
    return {
        "queries": draw_queries(jax.random.fold_in(streams_of[7], 71), 0),
        "key_rows": draw_key_rows(jax.random.fold_in(streams_of[7], 71), 0),
        "value_rows": normal_values(streams_of[2], (TOKENS, HEADS * HEAD_DIM), 1.0, 5.0, ((0, 64), (1, 4))),
        "out_grads": normal_values(streams_of[3], (TOKENS, HEADS * HEAD_DIM), 1.0, 5.0, ((0, 64), (1, 4))),
        "query_proj": normal_values(streams_of[4], (D, HEADS * HEAD_DIM), (HEADS * HEAD_DIM) ** -0.5, 0.25, ((1, 4),)),
        "key_proj": normal_values(streams_of[5], (D, HEADS * HEAD_DIM), (HEADS * HEAD_DIM) ** -0.5, 0.25, ((1, 4),)),
        "value_proj": normal_values(streams_of[6], (D, HEADS * HEAD_DIM), (HEADS * HEAD_DIM) ** -0.5, 0.25, ((1, 4),)),
    }


CONTRACT_LAST = (((1,), (1,)), ((), ()))
CONTRACT_FIRST = (((0,), (0,)), ((), ()))

def rope_tables(first_row, length, head_width):
    halfway = head_width // 2
    indices = jnp.arange(halfway).astype(jnp.float32)
    frequency = jnp.exp(indices * (-2.0 * math.log(10000.0) / head_width))
    positions = (first_row + jnp.arange(length, dtype=jnp.int32)).astype(jnp.float32)
    angles = positions[:, None] * frequency[None, :]
    cosine = jnp.cos(angles)
    sine_part = jnp.sin(angles)
    return (jnp.concatenate([cosine, cosine], axis=1), jnp.concatenate([sine_part, sine_part], axis=1))

def rope_back(gradient, cosine, sine_part):
    halfway = gradient.shape[1] // 2
    turned = gradient * sine_part
    return gradient * cosine + jnp.concatenate([turned[:, halfway:], -turned[:, :halfway]], axis=1)

def head_grads(queries, key_rows, value_rows, out_grads):
    length, head_width = queries.shape
    score_scale = 1.0 / math.sqrt(head_width)
    key_positions = jnp.arange(length, dtype=jnp.int32)

    def one_block(sums_state, block_index):
        d_keys, d_values = sums_state
        first_row = (block_index * TOK_DEV).astype(jnp.int32)
        query_block = lax.dynamic_slice_in_dim(queries, first_row, TOK_DEV, 0)
        grad_block = lax.dynamic_slice_in_dim(out_grads, first_row, TOK_DEV, 0)
        scores = lax.dot_general(query_block, key_rows, CONTRACT_LAST, preferred_element_type=jnp.float32) * score_scale
        positions = first_row + jnp.arange(TOK_DEV, dtype=jnp.int32)
        allowed = positions[:, None] >= key_positions[None, :]
        row_max = lax.optimization_barrier(jnp.max(jnp.where(allowed, scores, -jnp.inf), axis=1))
        shifted = jnp.where(allowed, jnp.exp(scores - row_max[:, None]), 0.0)
        log_total = row_max + jnp.log(lax.optimization_barrier(jnp.sum(shifted, axis=1)))
        weights = jnp.where(allowed, jnp.exp(scores - log_total[:, None]), 0.0)
        d_prob = lax.dot_general(grad_block, value_rows, CONTRACT_LAST, preferred_element_type=jnp.float32)
        grad_dot = lax.optimization_barrier(jnp.sum(weights * d_prob, axis=1))
        d_score = (weights * (d_prob - grad_dot[:, None]) * score_scale).astype(jnp.bfloat16)
        weights_low = weights.astype(jnp.bfloat16)
        d_query = jnp.dot(d_score, key_rows, preferred_element_type=jnp.float32)
        d_keys = d_keys + lax.dot_general(d_score, query_block, CONTRACT_FIRST, preferred_element_type=jnp.float32)
        d_values = d_values + lax.dot_general(weights_low, grad_block, CONTRACT_FIRST, preferred_element_type=jnp.float32)
        return ((d_keys, d_values), d_query)
    start_sums = (jnp.zeros((length, head_width), jnp.float32), jnp.zeros((length, head_width), jnp.float32))
    (d_keys, d_values), query_parts = lax.scan(one_block, start_sums, jnp.arange(length // TOK_DEV, dtype=jnp.int32))
    return (query_parts.reshape(length, head_width), d_keys, d_values)

def reference(queries, key_rows, value_rows, out_grads, query_proj, key_proj, value_proj):
    length = queries.shape[0]
    cosine, sine_part = rope_tables(0, length, HEAD_DIM)
    summed = jnp.zeros((length, D), jnp.float32)
    for head_index in range(HEADS):
        columns = slice(head_index * HEAD_DIM, (head_index + 1) * HEAD_DIM)
        d_query, d_keys, d_values = head_grads(queries[:, columns], key_rows[:, columns], value_rows[:, columns], out_grads[:, columns])
        query_in = rope_back(d_query, cosine, sine_part).astype(jnp.bfloat16)
        key_in = rope_back(d_keys, cosine, sine_part).astype(jnp.bfloat16)
        value_in = d_values.astype(jnp.bfloat16)
        summed = summed + lax.dot_general(query_in, query_proj[:, columns], CONTRACT_LAST, preferred_element_type=jnp.float32)
        summed = summed + lax.dot_general(key_in, key_proj[:, columns], CONTRACT_LAST, preferred_element_type=jnp.float32)
        summed = summed + lax.dot_general(value_in, value_proj[:, columns], CONTRACT_LAST, preferred_element_type=jnp.float32)
    return summed.astype(jnp.bfloat16)
```

```python
import functools
import math

import jax
import jax.numpy as jnp
from jax import lax
from jax.experimental import pallas as pl
from jax.experimental.pallas import tpu as pltpu
from jax.sharding import PartitionSpec as P

ROWS = 192
WIDTH = 128
QUARTER = 2 * ROWS
TILE = 8 * ROWS
SCALE = 1.0 / math.sqrt(WIDTH)
SCALE_LOG2 = SCALE / math.log(2.0)
LOWEST = -1e30
CONTRACT_LAST = (((1,), (1,)), ((), ()))
QUERY_SHIFTS = [(sx, se) for sx in range(4) for se in range(2)]
KEY_SHIFTS = [(st, sc) for sc in range(2) for st in range(4)]


def place(x, t, e, c):
    return 16 * (x % 4) + 4 * (t % 4) + 2 * e + c


def pairs_of(move):
    return [
        (place(x, t, e, c), place(*move(x, t, e, c)))
        for x in range(4)
        for t in range(4)
        for e in range(2)
        for c in range(2)
    ]


def to_query_member(value, sx, se):
    return lax.ppermute(value, "ctx", pairs_of(lambda x, t, e, c: (x + sx, t, e ^ se, c)))


def to_key_member(value, st):
    return lax.ppermute(value, "ctx", pairs_of(lambda x, t, e, c: (x + st, t + st, e, c)))


def to_other_core(value):
    return lax.ppermute(value, "ctx", pairs_of(lambda x, t, e, c: (x, t, e, 1 - c)))


def coordinates(ctx_index):
    return ctx_index // 16, (ctx_index // 4) % 4, (ctx_index // 2) % 2, ctx_index % 2


def slot_rows(slot):
    return pl.ds(pl.multiple_of(slot * ROWS, ROWS), ROWS)


def query_slot(ctx_index, sx, se, sign):
    x, _, e, _ = coordinates(ctx_index)
    return ((x + sign * sx + 4) % 4) * 2 + (e + se) % 2


def key_slot(ctx_index, st, sc, sign):
    x, _, _, c = coordinates(ctx_index)
    return ((x + sign * st + 4) % 4) * 2 + (c + sc) % 2


def diagonal_mask(ctx_index, quarter):
    x, t, e, c = coordinates(ctx_index)
    key_t = (quarter - x + t + 4) % 4
    key_first = (16 * quarter + 4 * key_t + 2 * e) * ROWS
    query_first = (16 * quarter + 4 * t + c) * ROWS
    keys = key_first + lax.broadcasted_iota(jnp.int32, (QUARTER, QUARTER), 0)
    columns = lax.broadcasted_iota(jnp.int32, (1, QUARTER), 1)
    queries = query_first + columns + jnp.where(columns >= ROWS, ROWS, 0)
    return queries >= keys


def chunk_scores(ctx_index, query_ref, key_ref, query_quarter, key_quarter):
    query_rows = pl.ds(query_quarter * QUARTER, QUARTER)
    key_rows = pl.ds(key_quarter * QUARTER, QUARTER)
    queries, out_grads = query_ref[query_rows, :WIDTH], query_ref[query_rows, WIDTH:]
    keys, values = key_ref[key_rows, :WIDTH], key_ref[key_rows, WIDTH:]
    scores = lax.dot_general(keys, queries, CONTRACT_LAST, preferred_element_type=jnp.float32)
    scores = scores * SCALE_LOG2
    if query_quarter == key_quarter:
        scores = jnp.where(diagonal_mask(ctx_index, query_quarter), scores, 2.0 * LOWEST)
    d_prob = lax.dot_general(values, out_grads, CONTRACT_LAST, preferred_element_type=jnp.float32)
    return queries, out_grads, scores, d_prob


def stats_kernel(ctx_ref, *refs):
    query_refs, key_refs, (query_ref, key_ref, stats_ref) = refs[:8], refs[8:16], refs[16:]
    ctx_index = ctx_ref[0]
    for (sx, se), ref in zip(QUERY_SHIFTS, query_refs):
        query_ref[slot_rows(query_slot(ctx_index, sx, se, -1)), :] = ref[...]
    for (st, sc), ref in zip(KEY_SHIFTS, key_refs):
        key_ref[slot_rows(key_slot(ctx_index, st, sc, -1)), :] = ref[...]
    for query_quarter in range(4):
        run_max = jnp.full((1, QUARTER), LOWEST, jnp.float32)
        run_total = jnp.zeros((1, QUARTER), jnp.float32)
        run_dot = jnp.zeros((1, QUARTER), jnp.float32)
        for key_quarter in range(query_quarter + 1):
            _, _, scores, d_prob = chunk_scores(
                ctx_index, query_ref, key_ref, query_quarter, key_quarter
            )
            new_max = jnp.maximum(run_max, jnp.max(scores, axis=0, keepdims=True))
            weights = jnp.exp2(scores - new_max)
            fade = jnp.exp2(run_max - new_max)
            run_total = run_total * fade + jnp.sum(weights, axis=0, keepdims=True)
            run_dot = run_dot * fade + jnp.sum(weights * d_prob, axis=0, keepdims=True)
            run_max = new_max
        some = run_total > 0.0
        log_total = jnp.where(some, run_max + jnp.log2(jnp.where(some, run_total, 1.0)), LOWEST)
        grad_dot = run_dot / jnp.where(some, run_total, 1.0)
        for part in range(3):
            row, lanes = 3 * query_quarter + part, slice(part * WIDTH, (part + 1) * WIDTH)
            stats_ref[row : row + 1, :] = log_total[:, lanes]
            stats_ref[12 + row : 13 + row, :] = grad_dot[:, lanes]


def grads_kernel(ctx_ref, query_ref, key_ref, *refs):
    stats_refs, query_out, own_out, other_out = refs[:8], refs[8:16], refs[16:20], refs[20:24]
    d_query_ref, d_pair_ref = refs[24:]
    ctx_index = ctx_ref[0]
    totals = [ref[0:12, :] for ref in stats_refs]
    top = functools.reduce(jnp.maximum, totals)
    shares = [jnp.exp2(total - top) for total in totals]
    share_sum = sum(shares)
    log_total = top + jnp.log2(share_sum)
    grad_dot = sum(share * ref[12:24, :] for share, ref in zip(shares, stats_refs)) / share_sum
    keys_turned = key_ref[:, :WIDTH].T
    d_keys, d_values = [None] * 4, [None] * 4
    for query_quarter in range(4):
        rows = [3 * query_quarter + part for part in range(3)]
        row_log = jnp.concatenate([log_total[row : row + 1, :] for row in rows], axis=1)
        row_dot = jnp.concatenate([grad_dot[row : row + 1, :] for row in rows], axis=1)
        d_query = None
        for key_quarter in range(query_quarter + 1):
            queries, out_grads, scores, d_prob = chunk_scores(
                ctx_index, query_ref, key_ref, query_quarter, key_quarter
            )
            weights = jnp.exp2(scores - row_log)
            d_score = (weights * (d_prob - row_dot)).astype(jnp.bfloat16)
            weights_low = weights.astype(jnp.bfloat16)
            d_key = jnp.dot(d_score, queries, preferred_element_type=jnp.float32)
            d_value = jnp.dot(weights_low, out_grads, preferred_element_type=jnp.float32)
            turned = keys_turned[:, key_quarter * QUARTER : (key_quarter + 1) * QUARTER]
            part = jnp.dot(turned, d_score, preferred_element_type=jnp.float32)
            key_rows = pl.ds(key_quarter * QUARTER, QUARTER)
            if query_quarter == key_quarter:
                d_pair_ref[key_rows, :WIDTH] = d_key
                d_pair_ref[key_rows, WIDTH:] = d_value
            else:
                d_pair_ref[key_rows, :WIDTH] += d_key
                d_pair_ref[key_rows, WIDTH:] += d_value
            d_query = part if d_query is None else d_query + part
        d_query_ref[pl.ds(query_quarter * QUARTER, QUARTER), :] = d_query.T * SCALE
    for (sx, se), ref in zip(QUERY_SHIFTS, query_out):
        ref[...] = d_query_ref[slot_rows(query_slot(ctx_index, sx, se, 1)), :].astype(ref.dtype)
    for (st, sc), ref in zip(KEY_SHIFTS, own_out + other_out):
        rows = slot_rows(key_slot(ctx_index, st, sc, 1))
        ref[:, :WIDTH] = (d_pair_ref[rows, :WIDTH] * SCALE).astype(ref.dtype)
        ref[:, WIDTH:] = d_pair_ref[rows, WIDTH:].astype(ref.dtype)


SCALAR = pl.BlockSpec(memory_space=pltpu.SMEM)
WHOLE = pl.BlockSpec(memory_space=pltpu.VMEM)


def tile_stats(ctx_index, query_blocks, key_blocks):
    tile = jax.ShapeDtypeStruct((TILE, 2 * WIDTH), jnp.bfloat16)
    return pl.pallas_call(
        stats_kernel,
        out_shape=[tile, tile, jax.ShapeDtypeStruct((24, WIDTH), jnp.float32)],
        in_specs=[SCALAR] + [WHOLE] * 16,
        out_specs=[WHOLE] * 3,
        compiler_params=pltpu.CompilerParams(vmem_limit_bytes=32 * 2**20),
        cost_estimate=pl.CostEstimate(
            flops=4 * 10 * QUARTER * QUARTER * WIDTH,
            bytes_accessed=4 * TILE * 4 * WIDTH,
            transcendentals=10 * QUARTER * QUARTER,
        ),
        name="tile_stats",
    )(ctx_index, *query_blocks, *key_blocks)


def tile_grads(ctx_index, queries, keys, stats):
    block = jax.ShapeDtypeStruct((ROWS, WIDTH), jnp.bfloat16)
    own = jax.ShapeDtypeStruct((ROWS, 2 * WIDTH), jnp.float32)
    other = jax.ShapeDtypeStruct((ROWS, 2 * WIDTH), jnp.bfloat16)
    first = jax.ShapeDtypeStruct((ROWS, WIDTH), jnp.float32)
    outs = pl.pallas_call(
        grads_kernel,
        out_shape=[first] + [block] * 7 + [own] * 4 + [other] * 4,
        in_specs=[SCALAR] + [WHOLE] * 10,
        out_specs=[WHOLE] * 16,
        scratch_shapes=[
            pltpu.VMEM((TILE, WIDTH), jnp.float32),
            pltpu.VMEM((TILE, 2 * WIDTH), jnp.float32),
        ],
        compiler_params=pltpu.CompilerParams(vmem_limit_bytes=32 * 2**20),
        cost_estimate=pl.CostEstimate(
            flops=10 * 10 * QUARTER * QUARTER * WIDTH,
            bytes_accessed=4 * TILE * 4 * WIDTH,
            transcendentals=10 * QUARTER * QUARTER,
        ),
        name="tile_grads",
    )(ctx_index, queries, keys, *stats)
    return outs[:8], outs[8:12], outs[12:]


def rope_tables(first_row, length, head_width):
    halfway = head_width // 2
    indices = jnp.arange(halfway).astype(jnp.float32)
    frequency = jnp.exp(indices * (-2.0 * math.log(10000.0) / head_width))
    positions = (first_row + jnp.arange(length, dtype=jnp.int32)).astype(jnp.float32)
    angles = positions[:, None] * frequency[None, :]
    cosine = jnp.cos(angles)
    sine_part = jnp.sin(angles)
    return (
        jnp.concatenate([cosine, cosine], axis=1),
        jnp.concatenate([sine_part, sine_part], axis=1),
    )


def rope_back(gradient, cosine, sine_part):
    halfway = gradient.shape[1] // 2
    turned = gradient * sine_part
    return gradient * cosine + jnp.concatenate([turned[:, halfway:], -turned[:, :halfway]], axis=1)


def to_head(value, step):
    count = lax.axis_size("head")
    return lax.ppermute(value, "head", [(h, (h + step) % count) for h in range(count)])


def shards(queries, key_rows, value_rows, out_grads, query_proj, key_proj, value_proj):
    ctx_index = lax.axis_index("ctx")
    head = lax.axis_index("head")
    scalar = ctx_index.astype(jnp.int32).reshape(1)
    query_pair = jnp.concatenate([queries, out_grads], axis=1)
    key_pair = jnp.concatenate([key_rows, value_rows], axis=1)
    near = [key_pair] + [to_key_member(key_pair, st) for st in range(1, 4)]
    query_blocks = [query_pair] + [to_query_member(query_pair, *s) for s in QUERY_SHIFTS[1:]]
    key_blocks = near + [to_other_core(block) for block in near]
    tile_queries, tile_keys, stats = tile_stats(scalar, query_blocks, key_blocks)

    columns = query_proj.shape[0] // 4
    weights = jnp.concatenate([query_proj, key_proj, value_proj], axis=1)

    def columns_of(owner):
        return lax.dynamic_slice_in_dim(weights, owner * columns, columns, 0)

    all_weights = [columns_of(head)] + [
        to_head(columns_of((head + step) % 4), step) for step in range(1, 4)
    ]

    all_stats = [stats] + [to_query_member(stats, *s) for s in QUERY_SHIFTS[1:]]
    d_query_parts, own_parts, other_parts = tile_grads(scalar, tile_queries, tile_keys, all_stats)

    d_query = d_query_parts[0]
    for shift, part in zip(QUERY_SHIFTS[1:], d_query_parts[1:]):
        d_query = d_query + to_query_member(part, *shift).astype(jnp.float32)
    from_core = [to_other_core(part) for part in other_parts]
    sums = [own + other.astype(jnp.float32) for own, other in zip(own_parts, from_core)]
    d_pair = sums[0]
    for st in range(1, 4):
        d_pair = d_pair + to_key_member(sums[st].astype(jnp.bfloat16), st).astype(jnp.float32)

    cosine, sine_part = rope_tables(ctx_index * ROWS, ROWS, WIDTH)
    query_in = rope_back(d_query, cosine, sine_part).astype(jnp.bfloat16)
    key_in = rope_back(d_pair[:, :WIDTH], cosine, sine_part).astype(jnp.bfloat16)
    value_in = d_pair[:, WIDTH:].astype(jnp.bfloat16)
    grads = jnp.concatenate([query_in, key_in, value_in], axis=1)
    total = None
    for step in range(4):
        part = grads if step == 0 else to_head(grads, step)
        term = lax.dot_general(
            part, all_weights[step], CONTRACT_LAST, preferred_element_type=jnp.float32
        )
        total = term if total is None else total + term
    return total.astype(jnp.bfloat16)


def solution(mesh):
    in_specs = (P("ctx", "head"),) * 4 + (P(None, "head"),) * 3
    return jax.shard_map(
        shards, mesh=mesh, in_specs=in_specs, out_specs=P("ctx", "head"), check_vma=False
    )
```

```python
import functools
import math

import jax
import jax.numpy as jnp
from jax import lax
from jax.experimental import pallas as pl
from jax.experimental.pallas import tpu as pltpu
from jax.sharding import PartitionSpec as P

ROWS = 192
WIDTH = 128
QUARTER = 2 * ROWS
TILE = 8 * ROWS
SCALE = 1.0 / math.sqrt(WIDTH)
SCALE_LOG2 = SCALE / math.log(2.0)
LOWEST = -1e30
CONTRACT_LAST = (((1,), (1,)), ((), ()))
QUERY_SHIFTS = [(sx, se) for sx in range(4) for se in range(2)]
KEY_SHIFTS = [(st, sc) for sc in range(2) for st in (0, 1, 3, 2)]
STEPS = (2, 1, 3)


def place(x, t, e, c):
    return 16 * (x % 4) + 4 * (t % 4) + 2 * e + c


def pairs_of(move):
    return [
        (place(x, t, e, c), place(*move(x, t, e, c)))
        for x in range(4)
        for t in range(4)
        for e in range(2)
        for c in range(2)
    ]


def to_neighbour(value):
    return to_query_member(value, 0, 1)


def to_query_member(value, sx, se):
    return lax.ppermute(value, "ctx", pairs_of(lambda x, t, e, c: (x + sx, t, e ^ se, c)))


def to_key_member(value, st):
    return lax.ppermute(value, "ctx", pairs_of(lambda x, t, e, c: (x + st, t + st, e, c)))


def to_other_core(value):
    return lax.ppermute(value, "ctx", pairs_of(lambda x, t, e, c: (x, t, e, 1 - c)))


QUERY_GROUPS = [
    [place(x, t, e, c) for x in range(4) for e in range(2)] for t in range(4) for c in range(2)
]


def exchange(value, groups):
    return lax.all_to_all(value, "ctx", 0, 0, axis_index_groups=groups, tiled=True)


def coordinates(ctx_index):
    return ctx_index // 16, (ctx_index // 4) % 4, (ctx_index // 2) % 2, ctx_index % 2


def slot_rows(slot):
    return pl.ds(pl.multiple_of(slot * ROWS, ROWS), ROWS)


def query_slot(ctx_index, sx, se, sign):
    x, _, e, _ = coordinates(ctx_index)
    return ((x + sign * sx + 4) % 4) * 2 + (e + se) % 2


def key_slot(ctx_index, st, sc, sign):
    x, _, _, c = coordinates(ctx_index)
    return ((x + sign * st + 4) % 4) * 2 + (c + sc) % 2


def diagonal_mask(ctx_index, quarter):
    x, t, e, c = coordinates(ctx_index)
    key_t = (quarter - x + t + 4) % 4
    key_first = (16 * quarter + 4 * key_t + 2 * e) * ROWS
    query_first = (16 * quarter + 4 * t + c) * ROWS
    keys = key_first + lax.broadcasted_iota(jnp.int32, (QUARTER, QUARTER), 0)
    columns = lax.broadcasted_iota(jnp.int32, (1, QUARTER), 1)
    queries = query_first + columns + jnp.where(columns >= ROWS, ROWS, 0)
    return queries >= keys


def chunk_scores(ctx_index, query_ref, key_ref, query_quarter, key_quarter):
    query_rows = pl.ds(query_quarter * QUARTER, QUARTER)
    key_rows = pl.ds(key_quarter * QUARTER, QUARTER)
    queries, out_grads = query_ref[query_rows, :WIDTH], query_ref[query_rows, WIDTH:]
    keys, values = key_ref[key_rows, :WIDTH], key_ref[key_rows, WIDTH:]
    scores = lax.dot_general(keys, queries, CONTRACT_LAST, preferred_element_type=jnp.float32)
    scores = scores * SCALE_LOG2
    if query_quarter == key_quarter:
        scores = jnp.where(diagonal_mask(ctx_index, query_quarter), scores, 2.0 * LOWEST)
    d_prob = lax.dot_general(values, out_grads, CONTRACT_LAST, preferred_element_type=jnp.float32)
    return queries, out_grads, scores, d_prob


def stats_kernel(ctx_ref, *refs):
    query_refs, key_refs, (query_ref, key_ref, stats_ref) = refs[:4], refs[4:12], refs[12:]
    ctx_index = ctx_ref[0]
    for sx, se in QUERY_SHIFTS:
        slot = slot_rows(query_slot(ctx_index, sx, se, -1))
        query_ref[slot, :] = query_refs[sx][se * ROWS : (se + 1) * ROWS, :]
    for (st, sc), ref in zip(KEY_SHIFTS, key_refs):
        key_ref[slot_rows(key_slot(ctx_index, st, sc, -1)), :] = ref[...]
    for query_quarter in range(4):
        run_max = jnp.full((1, QUARTER), LOWEST, jnp.float32)
        run_total = jnp.zeros((1, QUARTER), jnp.float32)
        run_dot = jnp.zeros((1, QUARTER), jnp.float32)
        for key_quarter in range(query_quarter + 1):
            _, _, scores, d_prob = chunk_scores(
                ctx_index, query_ref, key_ref, query_quarter, key_quarter
            )
            new_max = jnp.maximum(run_max, jnp.max(scores, axis=0, keepdims=True))
            weights = jnp.exp2(scores - new_max)
            fade = jnp.exp2(run_max - new_max)
            run_total = run_total * fade + jnp.sum(weights, axis=0, keepdims=True)
            run_dot = run_dot * fade + jnp.sum(weights * d_prob, axis=0, keepdims=True)
            run_max = new_max
        some = run_total > 0.0
        log_total = jnp.where(some, run_max + jnp.log2(jnp.where(some, run_total, 1.0)), LOWEST)
        grad_dot = run_dot / jnp.where(some, run_total, 1.0)
        for part in range(3):
            row, lanes = 3 * query_quarter + part, slice(part * WIDTH, (part + 1) * WIDTH)
            for copy in range(0, 8 * 24, 24):
                stats_ref[copy + row : copy + row + 1, :] = log_total[:, lanes]
                stats_ref[copy + 12 + row : copy + 13 + row, :] = grad_dot[:, lanes]


def grads_kernel(ctx_ref, query_ref, key_ref, stats_ref, *refs):
    query_out, own_out, other_out, d_query_ref, d_pair_ref = refs[:4], *refs[4:]
    ctx_index = ctx_ref[0]
    totals = [stats_ref[24 * i : 24 * i + 12, :] for i in range(8)]
    dots = [stats_ref[24 * i + 12 : 24 * i + 24, :] for i in range(8)]
    top = functools.reduce(jnp.maximum, totals)
    shares = [jnp.exp2(total - top) for total in totals]
    share_sum = sum(shares)
    log_total = top + jnp.log2(share_sum)
    grad_dot = sum(share * dot for share, dot in zip(shares, dots)) / share_sum
    keys_turned = key_ref[:, :WIDTH].T
    d_keys, d_values = [None] * 4, [None] * 4
    for query_quarter in range(4):
        rows = [3 * query_quarter + part for part in range(3)]
        row_log = jnp.concatenate([log_total[row : row + 1, :] for row in rows], axis=1)
        row_dot = jnp.concatenate([grad_dot[row : row + 1, :] for row in rows], axis=1)
        d_query = None
        for key_quarter in range(query_quarter + 1):
            queries, out_grads, scores, d_prob = chunk_scores(
                ctx_index, query_ref, key_ref, query_quarter, key_quarter
            )
            weights = jnp.exp2(scores - row_log)
            d_score = (weights * (d_prob - row_dot) * SCALE).astype(jnp.bfloat16)
            weights_low = weights.astype(jnp.bfloat16)
            d_key = jnp.dot(d_score, queries, preferred_element_type=jnp.float32)
            d_value = jnp.dot(weights_low, out_grads, preferred_element_type=jnp.float32)
            turned = keys_turned[:, key_quarter * QUARTER : (key_quarter + 1) * QUARTER]
            part = jnp.dot(turned, d_score, preferred_element_type=jnp.float32)
            key_rows = pl.ds(key_quarter * QUARTER, QUARTER)
            if query_quarter == key_quarter:
                d_pair_ref[key_rows, :WIDTH] = d_key
                d_pair_ref[key_rows, WIDTH:] = d_value
            else:
                d_pair_ref[key_rows, :WIDTH] += d_key
                d_pair_ref[key_rows, WIDTH:] += d_value
            d_query = part if d_query is None else d_query + part
        d_query_ref[pl.ds(query_quarter * QUARTER, QUARTER), :] = d_query.T
    for sx, se in QUERY_SHIFTS:
        slot = slot_rows(query_slot(ctx_index, sx, se, 1))
        part_rows = slice(se * ROWS, (se + 1) * ROWS)
        query_out[sx][part_rows, :] = d_query_ref[slot, :].astype(query_out[sx].dtype)
    for st, sc in KEY_SHIFTS:
        slot = slot_rows(key_slot(ctx_index, st, sc, 1))
        out = other_out if sc else own_out
        out[st * ROWS : (st + 1) * ROWS, :] = d_pair_ref[slot, :].astype(out.dtype)


def pack_kernel(core_ref, *refs):
    weights, blocks, (query_ref, key_ref, packed_ref, semaphores) = refs[:3], refs[3:7], refs[7:]
    half = packed_ref.shape[0] // 4
    copies = []
    for index, weight in enumerate(weights):
        for owner in range(4):
            first = pl.multiple_of((2 * owner + core_ref[0]) * half, half)
            source = weight.at[pl.ds(first, half), :]
            target = packed_ref.at[pl.ds(owner * half, half), pl.ds(index * WIDTH, WIDTH)]
            copies.append(pltpu.make_async_copy(source, target, semaphores.at[len(copies)]))
    for copy in copies:
        copy.start()
    query_ref[:, :WIDTH], query_ref[:, WIDTH:] = blocks[0][...], blocks[1][...]
    key_ref[:, :WIDTH], key_ref[:, WIDTH:] = blocks[2][...], blocks[3][...]
    for copy in copies:
        copy.wait()


SCALAR = pl.BlockSpec(memory_space=pltpu.SMEM)
WHOLE = pl.BlockSpec(memory_space=pltpu.VMEM)


def tile_stats(ctx_index, query_blocks, key_blocks):
    tile = jax.ShapeDtypeStruct((TILE, 2 * WIDTH), jnp.bfloat16)
    return pl.pallas_call(
        stats_kernel,
        out_shape=[tile, tile, jax.ShapeDtypeStruct((8 * 24, WIDTH), jnp.float32)],
        in_specs=[SCALAR] + [WHOLE] * 12,
        out_specs=[WHOLE] * 3,
        compiler_params=pltpu.CompilerParams(vmem_limit_bytes=32 * 2**20),
        cost_estimate=pl.CostEstimate(
            flops=4 * 10 * QUARTER * QUARTER * WIDTH,
            bytes_accessed=4 * TILE * 4 * WIDTH,
            transcendentals=10 * QUARTER * QUARTER,
        ),
        name="tile_stats",
    )(ctx_index, *query_blocks, *key_blocks)


def tile_grads(ctx_index, queries, keys, stats):
    own = jax.ShapeDtypeStruct((4 * ROWS, 2 * WIDTH), jnp.float32)
    other = jax.ShapeDtypeStruct((4 * ROWS, 2 * WIDTH), jnp.bfloat16)
    pair = jax.ShapeDtypeStruct((QUARTER, WIDTH), jnp.bfloat16)
    first = jax.ShapeDtypeStruct((QUARTER, WIDTH), jnp.float32)
    outs = pl.pallas_call(
        grads_kernel,
        out_shape=[first] + [pair] * 3 + [own, other],
        in_specs=[SCALAR] + [WHOLE] * 3,
        out_specs=[WHOLE] * 6,
        scratch_shapes=[
            pltpu.VMEM((TILE, WIDTH), jnp.float32),
            pltpu.VMEM((TILE, 2 * WIDTH), jnp.float32),
        ],
        compiler_params=pltpu.CompilerParams(vmem_limit_bytes=32 * 2**20),
        cost_estimate=pl.CostEstimate(
            flops=10 * 10 * QUARTER * QUARTER * WIDTH,
            bytes_accessed=4 * TILE * 4 * WIDTH,
            transcendentals=10 * QUARTER * QUARTER,
        ),
        name="tile_grads",
    )(ctx_index, queries, keys, stats)
    return outs[:4], outs[4], outs[5]


def pack(core, weights, blocks):
    rows = weights[0].shape[0] // 2
    pair = jax.ShapeDtypeStruct((ROWS, 2 * WIDTH), jnp.bfloat16)
    return pl.pallas_call(
        pack_kernel,
        out_shape=[pair, pair, jax.ShapeDtypeStruct((rows, 3 * WIDTH), jnp.bfloat16)],
        in_specs=[SCALAR] + [pl.BlockSpec(memory_space=pl.ANY)] * 3 + [WHOLE] * 4,
        out_specs=[WHOLE] * 3,
        scratch_shapes=[pltpu.SemaphoreType.DMA((12,))],
        compiler_params=pltpu.CompilerParams(vmem_limit_bytes=56 * 2**20),
        cost_estimate=pl.CostEstimate(
            flops=0, bytes_accessed=12 * rows * WIDTH, transcendentals=0
        ),
        name="pack",
    )(core, *weights, *blocks)


def rope_tables(first_row, length, head_width):
    halfway = head_width // 2
    indices = jnp.arange(halfway).astype(jnp.float32)
    frequency = jnp.exp(indices * (-2.0 * math.log(10000.0) / head_width))
    positions = (first_row + jnp.arange(length, dtype=jnp.int32)).astype(jnp.float32)
    angles = positions[:, None] * frequency[None, :]
    cosine = jnp.cos(angles)
    sine_part = jnp.sin(angles)
    return (
        jnp.concatenate([cosine, cosine], axis=1),
        jnp.concatenate([sine_part, sine_part], axis=1),
    )


def rope_back(gradient, cosine, sine_part):
    halfway = gradient.shape[1] // 2
    turned = gradient * sine_part
    return gradient * cosine + jnp.concatenate([turned[:, halfway:], -turned[:, :halfway]], axis=1)


def to_head(value, step):
    count = lax.axis_size("head")
    return lax.ppermute(value, "head", [(h, (h + step) % count) for h in range(count)])


def shards(queries, key_rows, value_rows, out_grads, query_proj, key_proj, value_proj):
    ctx_index = lax.axis_index("ctx")
    head = lax.axis_index("head")
    scalar = ctx_index.astype(jnp.int32).reshape(1)
    core = ctx_index % 2
    query_pair, key_pair, packed = pack(
        core.astype(jnp.int32).reshape(1),
        (query_proj, key_proj, value_proj),
        (queries, out_grads, key_rows, value_rows),
    )
    own_half = lax.all_to_all(packed, "head", 0, 0, tiled=True)
    query_near = to_neighbour(query_pair)
    near = {0: key_pair} | {st: to_key_member(key_pair, st) for st in STEPS}
    query_both = jnp.concatenate([query_pair, query_near], axis=0)
    query_blocks = {0: query_both} | {sx: to_query_member(query_both, sx, 0) for sx in STEPS}
    query_blocks = [query_blocks[sx] for sx in range(4)]
    near = [near[st] for st in (0, 1, 3, 2)]
    key_blocks = near + [to_other_core(block) for block in near]

    query_blocks, own_half = lax.optimization_barrier((query_blocks, own_half))
    tile_queries, tile_keys, stats = tile_stats(scalar, query_blocks, key_blocks)

    stats, own_half = lax.optimization_barrier((stats, own_half))
    other_half = to_other_core(own_half)
    all_stats = exchange(stats, QUERY_GROUPS)
    all_stats, other_half = lax.optimization_barrier((all_stats, other_half))
    d_query_parts, own_part, other_part = tile_grads(scalar, tile_queries, tile_keys, all_stats)

    sums = own_part + to_other_core(other_part).astype(jnp.float32)
    d_pair = sums[:ROWS]
    for st in STEPS:
        sent = sums[st * ROWS : (st + 1) * ROWS].astype(jnp.bfloat16)
        d_pair = d_pair + to_key_member(sent, st).astype(jnp.float32)
    d_query_both = d_query_parts[0]
    for sx in STEPS:
        d_query_both = d_query_both + to_query_member(d_query_parts[sx], sx, 0).astype(jnp.float32)
    d_query = d_query_both[:ROWS] + to_neighbour(
        d_query_both[ROWS:].astype(jnp.bfloat16)
    ).astype(jnp.float32)
    cosine, sine_part = rope_tables(ctx_index * ROWS, ROWS, WIDTH)
    query_in = rope_back(d_query, cosine, sine_part).astype(jnp.bfloat16)
    key_in = rope_back(d_pair[:, :WIDTH], cosine, sine_part).astype(jnp.bfloat16)
    value_in = d_pair[:, WIDTH:].astype(jnp.bfloat16)
    grads = jnp.concatenate([query_in, key_in, value_in], axis=1)
    half_columns = own_half.shape[0] // 4
    totals = None
    for step in range(4):
        part = grads if step == 0 else to_head(grads, step)
        first = ((head + 4 - step) % 4) * half_columns
        terms = [
            lax.dot_general(
                part,
                lax.dynamic_slice_in_dim(half, first, half_columns, 0),
                CONTRACT_LAST,
                preferred_element_type=jnp.float32,
            )
            for half in (own_half, other_half)
        ]
        totals = terms if step == 0 else [total + term for total, term in zip(totals, terms)]
    own_out, other_out = [total.astype(jnp.bfloat16) for total in totals]
    return jnp.where(
        core == 0,
        jnp.concatenate([own_out, other_out], axis=1),
        jnp.concatenate([other_out, own_out], axis=1),
    )


def solution(mesh):
    in_specs = (P("ctx", "head"),) * 4 + (P(None, "head"),) * 3
    return jax.shard_map(
        shards, mesh=mesh, in_specs=in_specs, out_specs=P("ctx", "head"), check_vma=False
    )
```

```python
import functools
import math

import jax
import jax.numpy as jnp
from jax import lax
from jax.experimental import pallas as pl
from jax.experimental.pallas import tpu as pltpu
from jax.sharding import PartitionSpec as P

ROWS = 192
WIDTH = 128
QUARTER = 2 * ROWS
TILE = 8 * ROWS
SCALE = 1.0 / math.sqrt(WIDTH)
SCALE_LOG2 = SCALE / math.log(2.0)
LOWEST = -1e30
CONTRACT_LAST = (((1,), (1,)), ((), ()))
QUERY_SHIFTS = [(sx, se) for sx in range(4) for se in range(2)]
KEY_SHIFTS = [(st, sc) for sc in range(2) for st in (0, 1, 3, 2)]
STEPS = (2, 1, 3)


def place(x, t, e, c):
    return 16 * (x % 4) + 4 * (t % 4) + 2 * e + c


def pairs_of(move):
    return [
        (place(x, t, e, c), place(*move(x, t, e, c)))
        for x in range(4)
        for t in range(4)
        for e in range(2)
        for c in range(2)
    ]


def to_neighbour(value):
    return to_query_member(value, 0, 1)


def to_query_member(value, sx, se):
    return lax.ppermute(value, "ctx", pairs_of(lambda x, t, e, c: (x ^ sx, t, e ^ se, c)))


def to_key_member(value, st):
    return lax.ppermute(value, "ctx", pairs_of(lambda x, t, e, c: (x - t + (t ^ st), t ^ st, e, c)))


def to_other_core(value):
    return lax.ppermute(value, "ctx", pairs_of(lambda x, t, e, c: (x, t, e, 1 - c)))


QUERY_GROUPS = [
    [place(x, t, e, c) for x in range(4) for e in range(2)] for t in range(4) for c in range(2)
]


def exchange(value, groups):
    return lax.all_to_all(value, "ctx", 0, 0, axis_index_groups=groups, tiled=True)


def coordinates(ctx_index):
    return ctx_index // 16, (ctx_index // 4) % 4, (ctx_index // 2) % 2, ctx_index % 2


def slot_rows(slot):
    return pl.ds(pl.multiple_of(slot * ROWS, ROWS), ROWS)


def query_slot(ctx_index, sx, se):
    x, _, e, _ = coordinates(ctx_index)
    return (x ^ sx) * 2 + (e ^ se)


def key_slot(ctx_index, st, sc):
    x, t, _, c = coordinates(ctx_index)
    return ((x - t + (t ^ st) + 4) % 4) * 2 + (c ^ sc)


def diagonal_mask(ctx_index, quarter):
    x, t, e, c = coordinates(ctx_index)
    key_t = (quarter - x + t + 4) % 4
    key_first = (16 * quarter + 4 * key_t + 2 * e) * ROWS
    query_first = (16 * quarter + 4 * t + c) * ROWS
    keys = key_first + lax.broadcasted_iota(jnp.int32, (QUARTER, QUARTER), 0)
    columns = lax.broadcasted_iota(jnp.int32, (1, QUARTER), 1)
    queries = query_first + columns + jnp.where(columns >= ROWS, ROWS, 0)
    return queries >= keys


def chunk_scores(ctx_index, query_ref, key_ref, query_quarter, key_quarter):
    query_rows = pl.ds(query_quarter * QUARTER, QUARTER)
    key_rows = pl.ds(key_quarter * QUARTER, QUARTER)
    queries, out_grads = query_ref[query_rows, :WIDTH], query_ref[query_rows, WIDTH:]
    keys, values = key_ref[key_rows, :WIDTH], key_ref[key_rows, WIDTH:]
    scores = lax.dot_general(keys, queries, CONTRACT_LAST, preferred_element_type=jnp.float32)
    scores = scores * SCALE_LOG2
    if query_quarter == key_quarter:
        scores = jnp.where(diagonal_mask(ctx_index, query_quarter), scores, 2.0 * LOWEST)
    d_prob = lax.dot_general(values, out_grads, CONTRACT_LAST, preferred_element_type=jnp.float32)
    return queries, out_grads, scores, d_prob


def stats_kernel(ctx_ref, *refs):
    query_refs, key_refs, (query_ref, key_ref, stats_ref) = refs[:4], refs[4:12], refs[12:]
    ctx_index = ctx_ref[0]
    for sx, se in QUERY_SHIFTS:
        slot = slot_rows(query_slot(ctx_index, sx, se))
        query_ref[slot, :] = query_refs[sx][se * ROWS : (se + 1) * ROWS, :]
    for (st, sc), ref in zip(KEY_SHIFTS, key_refs):
        key_ref[slot_rows(key_slot(ctx_index, st, sc)), :] = ref[...]
    for query_quarter in range(4):
        run_max = jnp.full((1, QUARTER), LOWEST, jnp.float32)
        run_total = jnp.zeros((1, QUARTER), jnp.float32)
        run_dot = jnp.zeros((1, QUARTER), jnp.float32)
        for key_quarter in range(query_quarter + 1):
            _, _, scores, d_prob = chunk_scores(
                ctx_index, query_ref, key_ref, query_quarter, key_quarter
            )
            new_max = jnp.maximum(run_max, jnp.max(scores, axis=0, keepdims=True))
            weights = jnp.exp2(scores - new_max)
            fade = jnp.exp2(run_max - new_max)
            run_total = run_total * fade + jnp.sum(weights, axis=0, keepdims=True)
            run_dot = run_dot * fade + jnp.sum(weights * d_prob, axis=0, keepdims=True)
            run_max = new_max
        some = run_total > 0.0
        log_total = jnp.where(some, run_max + jnp.log2(jnp.where(some, run_total, 1.0)), LOWEST)
        grad_dot = run_dot / jnp.where(some, run_total, 1.0)
        for part in range(3):
            row, lanes = 3 * query_quarter + part, slice(part * WIDTH, (part + 1) * WIDTH)
            for copy in range(0, 8 * 24, 24):
                stats_ref[copy + row : copy + row + 1, :] = log_total[:, lanes]
                stats_ref[copy + 12 + row : copy + 13 + row, :] = grad_dot[:, lanes]


def grads_kernel(ctx_ref, query_ref, key_ref, stats_ref, *refs):
    query_out, own_out, other_out, d_query_ref, d_pair_ref = refs[:4], *refs[4:]
    ctx_index = ctx_ref[0]
    totals = [stats_ref[24 * i : 24 * i + 12, :] for i in range(8)]
    dots = [stats_ref[24 * i + 12 : 24 * i + 24, :] for i in range(8)]
    top = functools.reduce(jnp.maximum, totals)
    shares = [jnp.exp2(total - top) for total in totals]
    share_sum = sum(shares)
    log_total = top + jnp.log2(share_sum)
    grad_dot = sum(share * dot for share, dot in zip(shares, dots)) / share_sum
    keys_turned = key_ref[:, :WIDTH].T
    d_keys, d_values = [None] * 4, [None] * 4
    for query_quarter in range(4):
        rows = [3 * query_quarter + part for part in range(3)]
        row_log = jnp.concatenate([log_total[row : row + 1, :] for row in rows], axis=1)
        row_dot = jnp.concatenate([grad_dot[row : row + 1, :] for row in rows], axis=1)
        d_query = None
        for key_quarter in range(query_quarter + 1):
            queries, out_grads, scores, d_prob = chunk_scores(
                ctx_index, query_ref, key_ref, query_quarter, key_quarter
            )
            weights = jnp.exp2(scores - row_log)
            d_score = (weights * (d_prob - row_dot) * SCALE).astype(jnp.bfloat16)
            weights_low = weights.astype(jnp.bfloat16)
            d_key = jnp.dot(d_score, queries, preferred_element_type=jnp.float32)
            d_value = jnp.dot(weights_low, out_grads, preferred_element_type=jnp.float32)
            turned = keys_turned[:, key_quarter * QUARTER : (key_quarter + 1) * QUARTER]
            part = jnp.dot(turned, d_score, preferred_element_type=jnp.float32)
            key_rows = pl.ds(key_quarter * QUARTER, QUARTER)
            if query_quarter == key_quarter:
                d_pair_ref[key_rows, :WIDTH] = d_key
                d_pair_ref[key_rows, WIDTH:] = d_value
            else:
                d_pair_ref[key_rows, :WIDTH] += d_key
                d_pair_ref[key_rows, WIDTH:] += d_value
            d_query = part if d_query is None else d_query + part
        d_query_ref[pl.ds(query_quarter * QUARTER, QUARTER), :] = d_query.T
    for sx, se in QUERY_SHIFTS:
        slot = slot_rows(query_slot(ctx_index, sx, se))
        part_rows = slice(se * ROWS, (se + 1) * ROWS)
        query_out[sx][part_rows, :] = d_query_ref[slot, :].astype(query_out[sx].dtype)
    for st, sc in KEY_SHIFTS:
        slot = slot_rows(key_slot(ctx_index, st, sc))
        out = other_out if sc else own_out
        out[st * ROWS : (st + 1) * ROWS, :] = d_pair_ref[slot, :].astype(out.dtype)


def pack_kernel(core_ref, *refs):
    sources, targets = refs[:7], refs[7:10]
    buffers, (in_sems, out_sems) = refs[10:13], refs[13:]
    half = targets[2].shape[0] // 4
    lanes = [pl.ds(index * WIDTH, WIDTH) for index in range(3)]
    parts = list(zip(targets, buffers))[:2]
    into = [
        [(sources[3 + 2 * pair + index], buffers[pair].at[:, lanes[index]]) for index in range(2)]
        for pair in range(2)
    ]
    for owner in range(4):
        first = pl.multiple_of((2 * owner + core_ref[0]) * half, half)
        rows = pl.ds(owner * half, half)
        parts.append((targets[2].at[rows, :], buffers[2].at[rows, :]))
        into.append(
            [
                (sources[index].at[pl.ds(first, half), :], buffers[2].at[rows, lanes[index]])
                for index in range(3)
            ]
        )
    loads, count = [], 0
    for part in into:
        loads.append([])
        for source, buffer in part:
            loads[-1].append(pltpu.make_async_copy(source, buffer, in_sems.at[count]))
            count += 1
    stores = [
        pltpu.make_async_copy(buffer, target, out_sems.at[index])
        for index, (target, buffer) in enumerate(parts)
    ]
    for part in loads:
        for load in part:
            load.start()
    for part, store in zip(loads, stores):
        for load in part:
            load.wait()
        store.start()
    for store in stores:
        store.wait()


SCALAR = pl.BlockSpec(memory_space=pltpu.SMEM)
WHOLE = pl.BlockSpec(memory_space=pltpu.VMEM)


def tile_stats(ctx_index, query_blocks, key_blocks):
    tile = jax.ShapeDtypeStruct((TILE, 2 * WIDTH), jnp.bfloat16)
    return pl.pallas_call(
        stats_kernel,
        out_shape=[tile, tile, jax.ShapeDtypeStruct((8 * 24, WIDTH), jnp.float32)],
        in_specs=[SCALAR] + [WHOLE] * 12,
        out_specs=[WHOLE] * 3,
        compiler_params=pltpu.CompilerParams(vmem_limit_bytes=32 * 2**20),
        cost_estimate=pl.CostEstimate(
            flops=4 * 10 * QUARTER * QUARTER * WIDTH,
            bytes_accessed=4 * TILE * 4 * WIDTH,
            transcendentals=10 * QUARTER * QUARTER,
        ),
        name="tile_stats",
    )(ctx_index, *query_blocks, *key_blocks)


def tile_grads(ctx_index, queries, keys, stats):
    own = jax.ShapeDtypeStruct((4 * ROWS, 2 * WIDTH), jnp.float32)
    other = jax.ShapeDtypeStruct((4 * ROWS, 2 * WIDTH), jnp.bfloat16)
    pair = jax.ShapeDtypeStruct((QUARTER, WIDTH), jnp.bfloat16)
    first = jax.ShapeDtypeStruct((QUARTER, WIDTH), jnp.float32)
    outs = pl.pallas_call(
        grads_kernel,
        out_shape=[first] + [pair] * 3 + [own, other],
        in_specs=[SCALAR] + [WHOLE] * 3,
        out_specs=[WHOLE] * 6,
        scratch_shapes=[
            pltpu.VMEM((TILE, WIDTH), jnp.float32),
            pltpu.VMEM((TILE, 2 * WIDTH), jnp.float32),
        ],
        compiler_params=pltpu.CompilerParams(vmem_limit_bytes=32 * 2**20),
        cost_estimate=pl.CostEstimate(
            flops=10 * 10 * QUARTER * QUARTER * WIDTH,
            bytes_accessed=4 * TILE * 4 * WIDTH,
            transcendentals=10 * QUARTER * QUARTER,
        ),
        name="tile_grads",
    )(ctx_index, queries, keys, stats)
    return outs[:4], outs[4], outs[5]


def pack(core, weights, blocks):
    rows = weights[0].shape[0] // 2
    shapes = [(ROWS, 2 * WIDTH), (ROWS, 2 * WIDTH), (rows, 3 * WIDTH)]
    anywhere = pl.BlockSpec(memory_space=pl.ANY)
    return pl.pallas_call(
        pack_kernel,
        out_shape=[jax.ShapeDtypeStruct(shape, jnp.bfloat16) for shape in shapes],
        in_specs=[SCALAR] + [anywhere] * 7,
        out_specs=[anywhere] * 3,
        scratch_shapes=[pltpu.VMEM(shape, jnp.bfloat16) for shape in shapes]
        + [pltpu.SemaphoreType.DMA((16,)), pltpu.SemaphoreType.DMA((6,))],
        compiler_params=pltpu.CompilerParams(vmem_limit_bytes=56 * 2**20),
        cost_estimate=pl.CostEstimate(
            flops=0, bytes_accessed=12 * rows * WIDTH, transcendentals=0
        ),
        name="pack",
    )(core, *weights, *blocks)


def rope_tables(first_row, length, head_width):
    halfway = head_width // 2
    indices = jnp.arange(halfway).astype(jnp.float32)
    frequency = jnp.exp(indices * (-2.0 * math.log(10000.0) / head_width))
    positions = (first_row + jnp.arange(length, dtype=jnp.int32)).astype(jnp.float32)
    angles = positions[:, None] * frequency[None, :]
    cosine = jnp.cos(angles)
    sine_part = jnp.sin(angles)
    return (
        jnp.concatenate([cosine, cosine], axis=1),
        jnp.concatenate([sine_part, sine_part], axis=1),
    )


def rope_back(gradient, cosine, sine_part):
    halfway = gradient.shape[1] // 2
    turned = gradient * sine_part
    return gradient * cosine + jnp.concatenate([turned[:, halfway:], -turned[:, :halfway]], axis=1)


def to_head(value, step):
    count = lax.axis_size("head")
    return lax.ppermute(value, "head", [(h, (h + step) % count) for h in range(count)])


def shards(queries, key_rows, value_rows, out_grads, query_proj, key_proj, value_proj):
    ctx_index = lax.axis_index("ctx")
    head = lax.axis_index("head")
    scalar = ctx_index.astype(jnp.int32).reshape(1)
    core = ctx_index % 2
    query_pair, key_pair, packed = pack(
        core.astype(jnp.int32).reshape(1),
        (query_proj, key_proj, value_proj),
        (queries, out_grads, key_rows, value_rows),
    )
    own_half = lax.all_to_all(packed, "head", 0, 0, tiled=True)
    query_near = to_neighbour(query_pair)
    near = {0: key_pair} | {st: to_key_member(key_pair, st) for st in STEPS}
    query_both = jnp.concatenate([query_pair, query_near], axis=0)
    query_blocks = {0: query_both} | {sx: to_query_member(query_both, sx, 0) for sx in STEPS}
    query_blocks = [query_blocks[sx] for sx in range(4)]
    near = [near[st] for st in (0, 1, 3, 2)]
    key_blocks = near + [to_other_core(block) for block in near]

    query_blocks, own_half = lax.optimization_barrier((query_blocks, own_half))
    tile_queries, tile_keys, stats = tile_stats(scalar, query_blocks, key_blocks)

    stats, own_half = lax.optimization_barrier((stats, own_half))
    other_half = to_other_core(own_half)
    all_stats = exchange(stats, QUERY_GROUPS)
    all_stats, other_half = lax.optimization_barrier((all_stats, other_half))
    d_query_parts, own_part, other_part = tile_grads(scalar, tile_queries, tile_keys, all_stats)

    sums = own_part + to_other_core(other_part).astype(jnp.float32)
    d_pair = sums[:ROWS]
    for st in STEPS:
        sent = sums[st * ROWS : (st + 1) * ROWS].astype(jnp.bfloat16)
        d_pair = d_pair + to_key_member(sent, st).astype(jnp.float32)
    d_query_both = d_query_parts[0]
    for sx in STEPS:
        d_query_both = d_query_both + to_query_member(d_query_parts[sx], sx, 0).astype(jnp.float32)
    d_query = d_query_both[:ROWS] + to_neighbour(
        d_query_both[ROWS:].astype(jnp.bfloat16)
    ).astype(jnp.float32)
    cosine, sine_part = rope_tables(ctx_index * ROWS, ROWS, WIDTH)
    query_in = rope_back(d_query, cosine, sine_part).astype(jnp.bfloat16)
    key_in = rope_back(d_pair[:, :WIDTH], cosine, sine_part).astype(jnp.bfloat16)
    value_in = d_pair[:, WIDTH:].astype(jnp.bfloat16)
    grads = jnp.concatenate([query_in, key_in, value_in], axis=1)
    half_columns = own_half.shape[0] // 4
    totals = None
    for step in range(4):
        part = grads if step == 0 else to_head(grads, step)
        first = ((head + 4 - step) % 4) * half_columns
        terms = [
            lax.dot_general(
                part,
                lax.dynamic_slice_in_dim(half, first, half_columns, 0),
                CONTRACT_LAST,
                preferred_element_type=jnp.float32,
            )
            for half in (own_half, other_half)
        ]
        totals = terms if step == 0 else [total + term for total, term in zip(totals, terms)]
    own_out, other_out = [total.astype(jnp.bfloat16) for total in totals]
    return jnp.where(
        core == 0,
        jnp.concatenate([own_out, other_out], axis=1),
        jnp.concatenate([other_out, own_out], axis=1),
    )


def solution(mesh):
    in_specs = (P("ctx", "head"),) * 4 + (P(None, "head"),) * 3
    return jax.shard_map(
        shards, mesh=mesh, in_specs=in_specs, out_specs=P("ctx", "head"), check_vma=False
    )
```

```python
import functools
import math

import jax
import jax.numpy as jnp
from jax import lax
from jax.experimental import pallas as pl
from jax.experimental.pallas import tpu as pltpu
from jax.sharding import PartitionSpec as P

ROWS = 192
WIDTH = 128
QUARTER = 2 * ROWS
TILE = 8 * ROWS
SCALE = 1.0 / math.sqrt(WIDTH)
SCALE_LOG2 = SCALE / math.log(2.0)
LOWEST = -1e30
CONTRACT_LAST = (((1,), (1,)), ((), ()))
QUERY_SHIFTS = [(sx, se) for sx in range(4) for se in range(2)]
KEY_SHIFTS = [(st, sc) for sc in range(2) for st in (0, 2, 1, 3)]
STEPS = (2, 1, 3)


def place(x, t, e, c):
    return 16 * (x % 4) + 4 * (t % 4) + 2 * e + c


def pairs_of(move):
    return [
        (place(x, t, e, c), place(*move(x, t, e, c)))
        for x in range(4)
        for t in range(4)
        for e in range(2)
        for c in range(2)
    ]


def to_neighbour(value):
    return to_query_member(value, 0, 1)


def to_query_member(value, sx, se):
    return lax.ppermute(value, "ctx", pairs_of(lambda x, t, e, c: (x ^ sx, t, e ^ se, c)))


def to_key_member(value, st):
    return lax.ppermute(value, "ctx", pairs_of(lambda x, t, e, c: (x - t + (t ^ st), t ^ st, e, c)))


def to_other_core(value):
    return lax.ppermute(value, "ctx", pairs_of(lambda x, t, e, c: (x, t, e, 1 - c)))


QUERY_GROUPS = [
    [place(x, t, e, c) for x in range(4) for e in range(2)] for t in range(4) for c in range(2)
]


def exchange(value, groups):
    return lax.all_to_all(value, "ctx", 0, 0, axis_index_groups=groups, tiled=True)


def coordinates(ctx_index):
    return ctx_index // 16, (ctx_index // 4) % 4, (ctx_index // 2) % 2, ctx_index % 2


def slot_rows(slot):
    return pl.ds(pl.multiple_of(slot * ROWS, ROWS), ROWS)


def query_slot(ctx_index, sx, se):
    x, _, e, _ = coordinates(ctx_index)
    return (x ^ sx) * 2 + (e ^ se)


def key_slot(ctx_index, st, sc):
    x, t, _, c = coordinates(ctx_index)
    return ((x - t + (t ^ st) + 4) % 4) * 2 + (c ^ sc)


def diagonal_mask(ctx_index, quarter):
    x, t, e, c = coordinates(ctx_index)
    key_t = (quarter - x + t + 4) % 4
    key_first = (16 * quarter + 4 * key_t + 2 * e) * ROWS
    query_first = (16 * quarter + 4 * t + c) * ROWS
    keys = key_first + lax.broadcasted_iota(jnp.int32, (QUARTER, QUARTER), 0)
    columns = lax.broadcasted_iota(jnp.int32, (1, QUARTER), 1)
    queries = query_first + columns + jnp.where(columns >= ROWS, ROWS, 0)
    return queries >= keys


def chunk_scores(ctx_index, query_ref, key_ref, query_quarter, key_quarter):
    query_rows = pl.ds(query_quarter * QUARTER, QUARTER)
    key_rows = pl.ds(key_quarter * QUARTER, QUARTER)
    queries, out_grads = query_ref[query_rows, :WIDTH], query_ref[query_rows, WIDTH:]
    keys, values = key_ref[key_rows, :WIDTH], key_ref[key_rows, WIDTH:]
    scores = lax.dot_general(keys, queries, CONTRACT_LAST, preferred_element_type=jnp.float32)
    scores = scores * SCALE_LOG2
    if query_quarter == key_quarter:
        scores = jnp.where(diagonal_mask(ctx_index, query_quarter), scores, 2.0 * LOWEST)
    d_prob = lax.dot_general(values, out_grads, CONTRACT_LAST, preferred_element_type=jnp.float32)
    return queries, out_grads, scores, d_prob


def band_scores(ctx_index, query_ref, key_ref, quarter):
    key_rows = pl.ds(quarter * QUARTER, QUARTER)
    queries, out_grads = query_ref[quarter * QUARTER :, :WIDTH], query_ref[quarter * QUARTER :, WIDTH:]
    keys, values = key_ref[key_rows, :WIDTH], key_ref[key_rows, WIDTH:]
    scores = lax.dot_general(keys, queries, CONTRACT_LAST, preferred_element_type=jnp.float32)
    scores = scores * SCALE_LOG2
    first = jnp.where(diagonal_mask(ctx_index, quarter), scores[:, :QUARTER], 2.0 * LOWEST)
    scores = first if quarter == 3 else jnp.concatenate([first, scores[:, QUARTER:]], axis=1)
    d_prob = lax.dot_general(values, out_grads, CONTRACT_LAST, preferred_element_type=jnp.float32)
    return queries, out_grads, scores, d_prob


def stats_kernel(ctx_ref, *refs):
    query_refs, key_refs, (query_ref, key_ref, stats_ref) = refs[:8], refs[8:16], refs[16:]
    ctx_index = ctx_ref[0]
    for (sx, se), ref in zip(QUERY_SHIFTS, query_refs):
        query_ref[slot_rows(query_slot(ctx_index, sx, se)), :] = ref[...]
    for (st, sc), ref in zip(KEY_SHIFTS, key_refs):
        key_ref[slot_rows(key_slot(ctx_index, st, sc)), :] = ref[...]
    for query_quarter in range(4):
        run_max = jnp.full((1, QUARTER), LOWEST, jnp.float32)
        run_total = jnp.zeros((1, QUARTER), jnp.float32)
        run_dot = jnp.zeros((1, QUARTER), jnp.float32)
        for key_quarter in range(query_quarter + 1):
            _, _, scores, d_prob = chunk_scores(
                ctx_index, query_ref, key_ref, query_quarter, key_quarter
            )
            new_max = jnp.maximum(run_max, jnp.max(scores, axis=0, keepdims=True))
            weights = jnp.exp2(scores - new_max)
            fade = jnp.exp2(run_max - new_max)
            run_total = run_total * fade + jnp.sum(weights, axis=0, keepdims=True)
            run_dot = run_dot * fade + jnp.sum(weights * d_prob, axis=0, keepdims=True)
            run_max = new_max
        some = run_total > 0.0
        log_total = jnp.where(some, run_max + jnp.log2(jnp.where(some, run_total, 1.0)), LOWEST)
        grad_dot = run_dot / jnp.where(some, run_total, 1.0)
        for part in range(3):
            row, lanes = 3 * query_quarter + part, slice(part * WIDTH, (part + 1) * WIDTH)
            for copy in range(0, 8 * 24, 24):
                stats_ref[copy + row : copy + row + 1, :] = log_total[:, lanes]
                stats_ref[copy + 12 + row : copy + 13 + row, :] = grad_dot[:, lanes]


def grads_kernel(ctx_ref, query_ref, key_ref, stats_ref, *refs):
    query_out, own_out, other_out, d_query_ref, d_pair_ref, turned_ref = refs[:4], *refs[4:]
    ctx_index = ctx_ref[0]
    totals = [stats_ref[24 * i : 24 * i + 12, :] for i in range(8)]
    dots = [stats_ref[24 * i + 12 : 24 * i + 24, :] for i in range(8)]
    top = functools.reduce(jnp.maximum, totals)
    shares = [jnp.exp2(total - top) for total in totals]
    share_sum = sum(shares)
    log_total = top + jnp.log2(share_sum)
    grad_dot = sum(share * dot for share, dot in zip(shares, dots)) / share_sum
    keys_turned = key_ref[:, :WIDTH].T
    row_log = jnp.concatenate([log_total[row : row + 1, :] for row in range(12)], axis=1)
    row_dot = jnp.concatenate([grad_dot[row : row + 1, :] for row in range(12)], axis=1)
    for quarter in range(4):
        first = quarter * QUARTER
        queries, out_grads, scores, d_prob = band_scores(ctx_index, query_ref, key_ref, quarter)
        weights = jnp.exp2(scores - row_log[:, first:])
        d_score = (weights * (d_prob - row_dot[:, first:]) * SCALE).astype(jnp.bfloat16)
        weights_low = weights.astype(jnp.bfloat16)
        key_rows = pl.ds(first, QUARTER)
        d_pair_ref[key_rows, :WIDTH] = jnp.dot(
            d_score, queries, preferred_element_type=jnp.float32
        )
        d_pair_ref[key_rows, WIDTH:] = jnp.dot(
            weights_low, out_grads, preferred_element_type=jnp.float32
        )
        turned = keys_turned[:, first : first + QUARTER]
        part = jnp.dot(turned, d_score, preferred_element_type=jnp.float32)
        if quarter == 0:
            turned_ref[...] = part
        else:
            turned_ref[:, first:] += part
    d_query_ref[...] = turned_ref[...].T
    for sx, se in QUERY_SHIFTS:
        slot = slot_rows(query_slot(ctx_index, sx, se))
        part_rows = slice(se * ROWS, (se + 1) * ROWS)
        query_out[sx][part_rows, :] = d_query_ref[slot, :].astype(query_out[sx].dtype)
    for st, sc in KEY_SHIFTS:
        slot = slot_rows(key_slot(ctx_index, st, sc))
        out = other_out if sc else own_out
        out[st * ROWS : (st + 1) * ROWS, :] = d_pair_ref[slot, :].astype(out.dtype)


def pack_kernel(core_ref, *refs):
    sources, targets = refs[:7], refs[7:10]
    buffers, (in_sems, out_sems) = refs[10:13], refs[13:]
    half = targets[2].shape[0] // 4
    lanes = [pl.ds(index * WIDTH, WIDTH) for index in range(3)]
    parts = list(zip(targets, buffers))[:2]
    into = [
        [(sources[3 + 2 * pair + index], buffers[pair].at[:, lanes[index]]) for index in range(2)]
        for pair in range(2)
    ]
    for owner in range(4):
        first = pl.multiple_of((2 * owner + core_ref[0]) * half, half)
        rows = pl.ds(owner * half, half)
        parts.append((targets[2].at[rows, :], buffers[2].at[rows, :]))
        into.append(
            [
                (sources[index].at[pl.ds(first, half), :], buffers[2].at[rows, lanes[index]])
                for index in range(3)
            ]
        )
    loads, count = [], 0
    for part in into:
        loads.append([])
        for source, buffer in part:
            loads[-1].append(pltpu.make_async_copy(source, buffer, in_sems.at[count]))
            count += 1
    stores = [
        pltpu.make_async_copy(buffer, target, out_sems.at[index])
        for index, (target, buffer) in enumerate(parts)
    ]
    for part in loads:
        for load in part:
            load.start()
    for part, store in zip(loads, stores):
        for load in part:
            load.wait()
        store.start()
    for store in stores:
        store.wait()


SCALAR = pl.BlockSpec(memory_space=pltpu.SMEM)
WHOLE = pl.BlockSpec(memory_space=pltpu.VMEM)


def tile_stats(ctx_index, query_blocks, key_blocks):
    tile = jax.ShapeDtypeStruct((TILE, 2 * WIDTH), jnp.bfloat16)
    return pl.pallas_call(
        stats_kernel,
        out_shape=[tile, tile, jax.ShapeDtypeStruct((8 * 24, WIDTH), jnp.float32)],
        in_specs=[SCALAR] + [WHOLE] * 16,
        out_specs=[WHOLE] * 3,
        compiler_params=pltpu.CompilerParams(vmem_limit_bytes=32 * 2**20),
        cost_estimate=pl.CostEstimate(
            flops=4 * 10 * QUARTER * QUARTER * WIDTH,
            bytes_accessed=4 * TILE * 4 * WIDTH,
            transcendentals=10 * QUARTER * QUARTER,
        ),
        name="tile_stats",
    )(ctx_index, *query_blocks, *key_blocks)


def tile_grads(ctx_index, queries, keys, stats):
    own = jax.ShapeDtypeStruct((4 * ROWS, 2 * WIDTH), jnp.float32)
    other = jax.ShapeDtypeStruct((4 * ROWS, 2 * WIDTH), jnp.bfloat16)
    pair = jax.ShapeDtypeStruct((QUARTER, WIDTH), jnp.bfloat16)
    first = jax.ShapeDtypeStruct((QUARTER, WIDTH), jnp.float32)
    outs = pl.pallas_call(
        grads_kernel,
        out_shape=[first] + [pair] * 3 + [own, other],
        in_specs=[SCALAR] + [WHOLE] * 3,
        out_specs=[WHOLE] * 6,
        scratch_shapes=[
            pltpu.VMEM((TILE, WIDTH), jnp.float32),
            pltpu.VMEM((TILE, 2 * WIDTH), jnp.float32),
            pltpu.VMEM((WIDTH, TILE), jnp.float32),
        ],
        compiler_params=pltpu.CompilerParams(vmem_limit_bytes=32 * 2**20),
        cost_estimate=pl.CostEstimate(
            flops=10 * 10 * QUARTER * QUARTER * WIDTH,
            bytes_accessed=4 * TILE * 4 * WIDTH,
            transcendentals=10 * QUARTER * QUARTER,
        ),
        name="tile_grads",
    )(ctx_index, queries, keys, stats)
    return outs[:4], outs[4], outs[5]


def pack(core, weights, blocks):
    rows = weights[0].shape[0] // 2
    shapes = [(ROWS, 2 * WIDTH), (ROWS, 2 * WIDTH), (rows, 3 * WIDTH)]
    anywhere = pl.BlockSpec(memory_space=pl.ANY)
    return pl.pallas_call(
        pack_kernel,
        out_shape=[jax.ShapeDtypeStruct(shape, jnp.bfloat16) for shape in shapes],
        in_specs=[SCALAR] + [anywhere] * 7,
        out_specs=[anywhere] * 3,
        scratch_shapes=[pltpu.VMEM(shape, jnp.bfloat16) for shape in shapes]
        + [pltpu.SemaphoreType.DMA((16,)), pltpu.SemaphoreType.DMA((6,))],
        compiler_params=pltpu.CompilerParams(vmem_limit_bytes=56 * 2**20),
        cost_estimate=pl.CostEstimate(
            flops=0, bytes_accessed=12 * rows * WIDTH, transcendentals=0
        ),
        name="pack",
    )(core, *weights, *blocks)


def rope_tables(first_row, length, head_width):
    halfway = head_width // 2
    indices = jnp.arange(halfway).astype(jnp.float32)
    frequency = jnp.exp(indices * (-2.0 * math.log(10000.0) / head_width))
    positions = (first_row + jnp.arange(length, dtype=jnp.int32)).astype(jnp.float32)
    angles = positions[:, None] * frequency[None, :]
    cosine = jnp.cos(angles)
    sine_part = jnp.sin(angles)
    return (
        jnp.concatenate([cosine, cosine], axis=1),
        jnp.concatenate([sine_part, sine_part], axis=1),
    )


def rope_back(gradient, cosine, sine_part):
    halfway = gradient.shape[1] // 2
    turned = gradient * sine_part
    return gradient * cosine + jnp.concatenate([turned[:, halfway:], -turned[:, :halfway]], axis=1)


def to_head(value, step):
    count = lax.axis_size("head")
    return lax.ppermute(value, "head", [(h, (h + step) % count) for h in range(count)])


def shards(queries, key_rows, value_rows, out_grads, query_proj, key_proj, value_proj):
    ctx_index = lax.axis_index("ctx")
    head = lax.axis_index("head")
    scalar = ctx_index.astype(jnp.int32).reshape(1)
    core = ctx_index % 2
    query_pair, key_pair, packed = pack(
        core.astype(jnp.int32).reshape(1),
        (query_proj, key_proj, value_proj),
        (queries, out_grads, key_rows, value_rows),
    )
    own_half = lax.all_to_all(packed, "head", 0, 0, tiled=True)
    query_near = to_neighbour(query_pair)
    near = {0: key_pair} | {st: to_key_member(key_pair, st) for st in STEPS}
    query_blocks = {(0, 0): query_pair, (0, 1): query_near}
    for se in range(2):
        for sx in STEPS:
            query_blocks[sx, se] = to_query_member(query_blocks[0, se], sx, 0)
    query_blocks = [query_blocks[shift] for shift in QUERY_SHIFTS]
    near = [near[st] for st in (0, 2, 1, 3)]
    key_blocks = near + [to_other_core(block) for block in near]

    query_blocks, own_half = lax.optimization_barrier((query_blocks, own_half))
    tile_queries, tile_keys, stats = tile_stats(scalar, query_blocks, key_blocks)

    stats, own_half = lax.optimization_barrier((stats, own_half))
    other_half = to_other_core(own_half)
    all_stats = exchange(stats, QUERY_GROUPS)
    all_stats, other_half = lax.optimization_barrier((all_stats, other_half))
    d_query_parts, own_part, other_part = tile_grads(scalar, tile_queries, tile_keys, all_stats)

    sums = own_part + to_other_core(other_part).astype(jnp.float32)
    d_pair = sums[:ROWS]
    for st in STEPS:
        sent = sums[st * ROWS : (st + 1) * ROWS].astype(jnp.bfloat16)
        d_pair = d_pair + to_key_member(sent, st).astype(jnp.float32)
    d_query_both = d_query_parts[0]
    for sx in STEPS:
        d_query_both = d_query_both + to_query_member(d_query_parts[sx], sx, 0).astype(jnp.float32)
    d_query = d_query_both[:ROWS] + to_neighbour(
        d_query_both[ROWS:].astype(jnp.bfloat16)
    ).astype(jnp.float32)
    cosine, sine_part = rope_tables(ctx_index * ROWS, ROWS, WIDTH)
    query_in = rope_back(d_query, cosine, sine_part).astype(jnp.bfloat16)
    key_in = rope_back(d_pair[:, :WIDTH], cosine, sine_part).astype(jnp.bfloat16)
    value_in = d_pair[:, WIDTH:].astype(jnp.bfloat16)
    grads = jnp.concatenate([query_in, key_in, value_in], axis=1)
    half_columns = own_half.shape[0] // 4
    totals = None
    for step in range(4):
        part = grads if step == 0 else to_head(grads, step)
        first = ((head + 4 - step) % 4) * half_columns
        terms = [
            lax.dot_general(
                part,
                lax.dynamic_slice_in_dim(half, first, half_columns, 0),
                CONTRACT_LAST,
                preferred_element_type=jnp.float32,
            )
            for half in (own_half, other_half)
        ]
        totals = terms if step == 0 else [total + term for total, term in zip(totals, terms)]
    own_out, other_out = [total.astype(jnp.bfloat16) for total in totals]
    return jnp.where(
        core == 0,
        jnp.concatenate([own_out, other_out], axis=1),
        jnp.concatenate([other_out, own_out], axis=1),
    )


def solution(mesh):
    in_specs = (P("ctx", "head"),) * 4 + (P(None, "head"),) * 3
    return jax.shard_map(
        shards, mesh=mesh, in_specs=in_specs, out_specs=P("ctx", "head"), check_vma=False
    )
```

```python
import functools
import math

import jax
import jax.numpy as jnp
from jax import lax
from jax.experimental import pallas as pl
from jax.experimental.pallas import tpu as pltpu
from jax.sharding import PartitionSpec as P

ROWS = 192
WIDTH = 128
QUARTER = 2 * ROWS
TILE = 8 * ROWS
SCALE = 1.0 / math.sqrt(WIDTH)
SCALE_LOG2 = SCALE / math.log(2.0)
LOWEST = -1e30
CONTRACT_LAST = (((1,), (1,)), ((), ()))
QUERY_SHIFTS = [(sx, se) for sx in range(4) for se in range(2)]
KEY_SHIFTS = [(st, sc) for sc in range(2) for st in (0, 2, 1, 3)]
STEPS = (2, 1, 3)


def place(x, t, e, c):
    return 16 * (x % 4) + 4 * (t % 4) + 2 * e + c


def pairs_of(move):
    return [
        (place(x, t, e, c), place(*move(x, t, e, c)))
        for x in range(4)
        for t in range(4)
        for e in range(2)
        for c in range(2)
    ]


def to_neighbour(value):
    return to_query_member(value, 0, 1)


def to_query_member(value, sx, se):
    return lax.ppermute(value, "ctx", pairs_of(lambda x, t, e, c: (x ^ sx, t, e ^ se, c)))


def to_key_member(value, st):
    return lax.ppermute(value, "ctx", pairs_of(lambda x, t, e, c: (x - t + (t ^ st), t ^ st, e, c)))


def to_other_core(value):
    return lax.ppermute(value, "ctx", pairs_of(lambda x, t, e, c: (x, t, e, 1 - c)))


QUERY_GROUPS = [
    [place(x, t, e, c) for x in range(4) for e in range(2)] for t in range(4) for c in range(2)
]


def exchange(value, groups):
    return lax.all_to_all(value, "ctx", 0, 0, axis_index_groups=groups, tiled=True)


def coordinates(ctx_index):
    return ctx_index // 16, (ctx_index // 4) % 4, (ctx_index // 2) % 2, ctx_index % 2


def slot_rows(slot):
    return pl.ds(pl.multiple_of(slot * ROWS, ROWS), ROWS)


def query_slot(ctx_index, sx, se):
    x, _, e, _ = coordinates(ctx_index)
    return (x ^ sx) * 2 + (e ^ se)


def key_slot(ctx_index, st, sc):
    x, t, _, c = coordinates(ctx_index)
    return ((x - t + (t ^ st) + 4) % 4) * 2 + (c ^ sc)


def diagonal_mask(ctx_index, quarter):
    x, t, e, c = coordinates(ctx_index)
    key_t = (quarter - x + t + 4) % 4
    key_first = (16 * quarter + 4 * key_t + 2 * e) * ROWS
    query_first = (16 * quarter + 4 * t + c) * ROWS
    keys = key_first + lax.broadcasted_iota(jnp.int32, (QUARTER, QUARTER), 0)
    columns = lax.broadcasted_iota(jnp.int32, (1, QUARTER), 1)
    queries = query_first + columns + jnp.where(columns >= ROWS, ROWS, 0)
    return queries >= keys


def chunk_scores(ctx_index, query_ref, key_ref, query_quarter, key_quarter):
    query_rows = pl.ds(query_quarter * QUARTER, QUARTER)
    key_rows = pl.ds(key_quarter * QUARTER, QUARTER)
    queries, out_grads = query_ref[query_rows, :WIDTH], query_ref[query_rows, WIDTH:]
    keys, values = key_ref[key_rows, :WIDTH], key_ref[key_rows, WIDTH:]
    scores = lax.dot_general(keys, queries, CONTRACT_LAST, preferred_element_type=jnp.float32)
    scores = scores * SCALE_LOG2
    if query_quarter == key_quarter:
        scores = jnp.where(diagonal_mask(ctx_index, query_quarter), scores, 2.0 * LOWEST)
    d_prob = lax.dot_general(values, out_grads, CONTRACT_LAST, preferred_element_type=jnp.float32)
    return queries, out_grads, scores, d_prob


def band_scores(ctx_index, query_ref, key_ref, quarter):
    key_rows = pl.ds(quarter * QUARTER, QUARTER)
    queries, out_grads = query_ref[quarter * QUARTER :, :WIDTH], query_ref[quarter * QUARTER :, WIDTH:]
    keys, values = key_ref[key_rows, :WIDTH], key_ref[key_rows, WIDTH:]
    scores = lax.dot_general(keys, queries, CONTRACT_LAST, preferred_element_type=jnp.float32)
    scores = scores * SCALE_LOG2
    first = jnp.where(diagonal_mask(ctx_index, quarter), scores[:, :QUARTER], 2.0 * LOWEST)
    scores = first if quarter == 3 else jnp.concatenate([first, scores[:, QUARTER:]], axis=1)
    d_prob = lax.dot_general(values, out_grads, CONTRACT_LAST, preferred_element_type=jnp.float32)
    return queries, out_grads, scores, d_prob


def stats_kernel(ctx_ref, *refs):
    query_refs, key_refs, (query_ref, key_ref, stats_ref) = refs[:8], refs[8:16], refs[16:]
    ctx_index = ctx_ref[0]
    for (sx, se), ref in zip(QUERY_SHIFTS, query_refs):
        query_ref[slot_rows(query_slot(ctx_index, sx, se)), :] = ref[...]
    for (st, sc), ref in zip(KEY_SHIFTS, key_refs):
        key_ref[slot_rows(key_slot(ctx_index, st, sc)), :] = ref[...]
    for query_quarter in range(4):
        run_max = jnp.full((1, QUARTER), LOWEST, jnp.float32)
        run_total = jnp.zeros((1, QUARTER), jnp.float32)
        run_dot = jnp.zeros((1, QUARTER), jnp.float32)
        for key_quarter in range(query_quarter + 1):
            _, _, scores, d_prob = chunk_scores(
                ctx_index, query_ref, key_ref, query_quarter, key_quarter
            )
            new_max = jnp.maximum(run_max, jnp.max(scores, axis=0, keepdims=True))
            weights = jnp.exp2(scores - new_max)
            fade = jnp.exp2(run_max - new_max)
            run_total = run_total * fade + jnp.sum(weights, axis=0, keepdims=True)
            run_dot = run_dot * fade + jnp.sum(weights * d_prob, axis=0, keepdims=True)
            run_max = new_max
        some = run_total > 0.0
        log_total = jnp.where(some, run_max + jnp.log2(jnp.where(some, run_total, 1.0)), LOWEST)
        grad_dot = run_dot / jnp.where(some, run_total, 1.0)
        for part in range(3):
            row, lanes = 3 * query_quarter + part, slice(part * WIDTH, (part + 1) * WIDTH)
            for copy in range(0, 8 * 24, 24):
                stats_ref[copy + row : copy + row + 1, :] = log_total[:, lanes]
                stats_ref[copy + 12 + row : copy + 13 + row, :] = grad_dot[:, lanes]


def grads_kernel(ctx_ref, query_ref, key_ref, stats_ref, *refs):
    query_out, own_out, other_out, d_query_ref, d_pair_ref, turned_ref = refs[:4], *refs[4:]
    ctx_index = ctx_ref[0]
    totals = [stats_ref[24 * i : 24 * i + 12, :] for i in range(8)]
    dots = [stats_ref[24 * i + 12 : 24 * i + 24, :] for i in range(8)]
    top = functools.reduce(jnp.maximum, totals)
    shares = [jnp.exp2(total - top) for total in totals]
    share_sum = sum(shares)
    log_total = top + jnp.log2(share_sum)
    grad_dot = sum(share * dot for share, dot in zip(shares, dots)) / share_sum
    keys_turned = key_ref[:, :WIDTH].T
    row_log = jnp.concatenate([log_total[row : row + 1, :] for row in range(12)], axis=1)
    row_dot = jnp.concatenate([grad_dot[row : row + 1, :] for row in range(12)], axis=1)
    for quarter in range(4):
        first = quarter * QUARTER
        queries, out_grads, scores, d_prob = band_scores(ctx_index, query_ref, key_ref, quarter)
        weights = jnp.exp2(scores - row_log[:, first:])
        d_score = (weights * (d_prob - row_dot[:, first:]) * SCALE).astype(jnp.bfloat16)
        weights_low = weights.astype(jnp.bfloat16)
        key_rows = pl.ds(first, QUARTER)
        d_pair_ref[key_rows, :WIDTH] = jnp.dot(
            d_score, queries, preferred_element_type=jnp.float32
        )
        d_pair_ref[key_rows, WIDTH:] = jnp.dot(
            weights_low, out_grads, preferred_element_type=jnp.float32
        )
        turned = keys_turned[:, first : first + QUARTER]
        part = jnp.dot(turned, d_score, preferred_element_type=jnp.float32)
        if quarter == 0:
            turned_ref[...] = part
        else:
            turned_ref[:, first:] += part
    d_query_ref[...] = turned_ref[...].T
    for sx, se in QUERY_SHIFTS:
        slot = slot_rows(query_slot(ctx_index, sx, se))
        part_rows = slice(se * ROWS, (se + 1) * ROWS)
        query_out[sx][part_rows, :] = d_query_ref[slot, :].astype(query_out[sx].dtype)
    for st, sc in KEY_SHIFTS:
        slot = slot_rows(key_slot(ctx_index, st, sc))
        out = other_out if sc else own_out
        out[st * ROWS : (st + 1) * ROWS, :] = d_pair_ref[slot, :].astype(out.dtype)


def pack_kernel(core_ref, *refs):
    sources, targets = refs[:7], refs[7:10]
    buffers, (in_sems, out_sems) = refs[10:13], refs[13:]
    half = targets[2].shape[0] // 4
    lanes = [pl.ds(index * WIDTH, WIDTH) for index in range(3)]
    parts, into = [], []
    for owner in range(4):
        first = pl.multiple_of((2 * owner + core_ref[0]) * half, half)
        rows = pl.ds(owner * half, half)
        parts.append((targets[2].at[rows, :], buffers[2].at[rows, :]))
        into.append(
            [
                (sources[index].at[pl.ds(first, half), :], buffers[2].at[rows, lanes[index]])
                for index in range(3)
            ]
        )
    parts += list(zip(targets, buffers))[:2]
    into += [
        [(sources[3 + 2 * pair + index], buffers[pair].at[:, lanes[index]]) for index in range(2)]
        for pair in range(2)
    ]
    loads, count = [], 0
    for part in into:
        loads.append([])
        for source, buffer in part:
            loads[-1].append(pltpu.make_async_copy(source, buffer, in_sems.at[count]))
            count += 1
    stores = [
        pltpu.make_async_copy(buffer, target, out_sems.at[index])
        for index, (target, buffer) in enumerate(parts)
    ]
    for part in loads:
        for load in part:
            load.start()
    for part, store in zip(loads, stores):
        for load in part:
            load.wait()
        store.start()
    for store in stores:
        store.wait()


SCALAR = pl.BlockSpec(memory_space=pltpu.SMEM)
WHOLE = pl.BlockSpec(memory_space=pltpu.VMEM)


def tile_stats(ctx_index, query_blocks, key_blocks):
    tile = jax.ShapeDtypeStruct((TILE, 2 * WIDTH), jnp.bfloat16)
    return pl.pallas_call(
        stats_kernel,
        out_shape=[tile, tile, jax.ShapeDtypeStruct((8 * 24, WIDTH), jnp.float32)],
        in_specs=[SCALAR] + [WHOLE] * 16,
        out_specs=[WHOLE] * 3,
        compiler_params=pltpu.CompilerParams(vmem_limit_bytes=32 * 2**20),
        cost_estimate=pl.CostEstimate(
            flops=4 * 10 * QUARTER * QUARTER * WIDTH,
            bytes_accessed=4 * TILE * 4 * WIDTH,
            transcendentals=10 * QUARTER * QUARTER,
        ),
        name="tile_stats",
    )(ctx_index, *query_blocks, *key_blocks)


def tile_grads(ctx_index, queries, keys, stats):
    own = jax.ShapeDtypeStruct((4 * ROWS, 2 * WIDTH), jnp.float32)
    other = jax.ShapeDtypeStruct((4 * ROWS, 2 * WIDTH), jnp.bfloat16)
    pair = jax.ShapeDtypeStruct((QUARTER, WIDTH), jnp.bfloat16)
    first = jax.ShapeDtypeStruct((QUARTER, WIDTH), jnp.float32)
    outs = pl.pallas_call(
        grads_kernel,
        out_shape=[first] + [pair] * 3 + [own, other],
        in_specs=[SCALAR] + [WHOLE] * 3,
        out_specs=[WHOLE] * 6,
        scratch_shapes=[
            pltpu.VMEM((TILE, WIDTH), jnp.float32),
            pltpu.VMEM((TILE, 2 * WIDTH), jnp.float32),
            pltpu.VMEM((WIDTH, TILE), jnp.float32),
        ],
        compiler_params=pltpu.CompilerParams(vmem_limit_bytes=32 * 2**20),
        cost_estimate=pl.CostEstimate(
            flops=10 * 10 * QUARTER * QUARTER * WIDTH,
            bytes_accessed=4 * TILE * 4 * WIDTH,
            transcendentals=10 * QUARTER * QUARTER,
        ),
        name="tile_grads",
    )(ctx_index, queries, keys, stats)
    return outs[:4], outs[4], outs[5]


def pack(core, weights, blocks):
    rows = weights[0].shape[0] // 2
    shapes = [(ROWS, 2 * WIDTH), (ROWS, 2 * WIDTH), (rows, 3 * WIDTH)]
    anywhere = pl.BlockSpec(memory_space=pl.ANY)
    return pl.pallas_call(
        pack_kernel,
        out_shape=[jax.ShapeDtypeStruct(shape, jnp.bfloat16) for shape in shapes],
        in_specs=[SCALAR] + [anywhere] * 7,
        out_specs=[anywhere] * 3,
        scratch_shapes=[pltpu.VMEM(shape, jnp.bfloat16) for shape in shapes]
        + [pltpu.SemaphoreType.DMA((16,)), pltpu.SemaphoreType.DMA((6,))],
        compiler_params=pltpu.CompilerParams(vmem_limit_bytes=56 * 2**20),
        cost_estimate=pl.CostEstimate(
            flops=0, bytes_accessed=12 * rows * WIDTH, transcendentals=0
        ),
        name="pack",
    )(core, *weights, *blocks)


def rope_tables(first_row, length, head_width):
    halfway = head_width // 2
    indices = jnp.arange(halfway).astype(jnp.float32)
    frequency = jnp.exp(indices * (-2.0 * math.log(10000.0) / head_width))
    positions = (first_row + jnp.arange(length, dtype=jnp.int32)).astype(jnp.float32)
    angles = positions[:, None] * frequency[None, :]
    cosine = jnp.cos(angles)
    sine_part = jnp.sin(angles)
    return (
        jnp.concatenate([cosine, cosine], axis=1),
        jnp.concatenate([sine_part, sine_part], axis=1),
    )


def rope_back(gradient, cosine, sine_part):
    halfway = gradient.shape[1] // 2
    turned = gradient * sine_part
    return gradient * cosine + jnp.concatenate([turned[:, halfway:], -turned[:, :halfway]], axis=1)


def to_head(value, step):
    count = lax.axis_size("head")
    return lax.ppermute(value, "head", [(h, (h + step) % count) for h in range(count)])


def shards(queries, key_rows, value_rows, out_grads, query_proj, key_proj, value_proj):
    ctx_index = lax.axis_index("ctx")
    head = lax.axis_index("head")
    scalar = ctx_index.astype(jnp.int32).reshape(1)
    core = ctx_index % 2
    query_pair, key_pair, packed = pack(
        core.astype(jnp.int32).reshape(1),
        (query_proj, key_proj, value_proj),
        (queries, out_grads, key_rows, value_rows),
    )
    own_half = lax.all_to_all(packed, "head", 0, 0, tiled=True)
    query_near = to_neighbour(query_pair)
    near = {0: key_pair} | {st: to_key_member(key_pair, st) for st in STEPS}
    query_blocks = {(0, 0): query_pair, (0, 1): query_near}
    for se in range(2):
        for sx in STEPS:
            query_blocks[sx, se] = to_query_member(query_blocks[0, se], sx, 0)
    query_blocks = [query_blocks[shift] for shift in QUERY_SHIFTS]
    near = [near[st] for st in (0, 2, 1, 3)]
    key_blocks = near + [to_other_core(block) for block in near]

    query_blocks, own_half = lax.optimization_barrier((query_blocks, own_half))
    tile_queries, tile_keys, stats = tile_stats(scalar, query_blocks, key_blocks)

    stats, own_half = lax.optimization_barrier((stats, own_half))
    other_half = to_other_core(own_half)
    all_stats = exchange(stats, QUERY_GROUPS)
    all_stats, other_half = lax.optimization_barrier((all_stats, other_half))
    d_query_parts, own_part, other_part = tile_grads(scalar, tile_queries, tile_keys, all_stats)

    from_core = to_other_core(other_part)
    blocks = [slice(st * ROWS, (st + 1) * ROWS) for st in range(4)]
    sums = [own_part[rows] + from_core[rows].astype(jnp.float32) for rows in blocks]
    d_pair = sums[0]
    for st in STEPS:
        d_pair = d_pair + to_key_member(sums[st].astype(jnp.bfloat16), st).astype(jnp.float32)
    d_query_both = d_query_parts[0]
    for sx in STEPS:
        d_query_both = d_query_both + to_query_member(d_query_parts[sx], sx, 0).astype(jnp.float32)
    d_query = d_query_both[:ROWS] + to_neighbour(
        d_query_both[ROWS:].astype(jnp.bfloat16)
    ).astype(jnp.float32)
    cosine, sine_part = rope_tables(ctx_index * ROWS, ROWS, WIDTH)
    query_in = rope_back(d_query, cosine, sine_part).astype(jnp.bfloat16)
    key_in = rope_back(d_pair[:, :WIDTH], cosine, sine_part).astype(jnp.bfloat16)
    value_in = d_pair[:, WIDTH:].astype(jnp.bfloat16)
    grads = jnp.concatenate([query_in, key_in, value_in], axis=1)
    half_columns = own_half.shape[0] // 4
    totals = None
    for step in range(4):
        part = grads if step == 0 else to_head(grads, step)
        first = ((head + 4 - step) % 4) * half_columns
        terms = [
            lax.dot_general(
                part,
                lax.dynamic_slice_in_dim(half, first, half_columns, 0),
                CONTRACT_LAST,
                preferred_element_type=jnp.float32,
            )
            for half in (own_half, other_half)
        ]
        totals = terms if step == 0 else [total + term for total, term in zip(totals, terms)]
    own_out, other_out = [total.astype(jnp.bfloat16) for total in totals]
    return jnp.where(
        core == 0,
        jnp.concatenate([own_out, other_out], axis=1),
        jnp.concatenate([other_out, own_out], axis=1),
    )


def solution(mesh):
    in_specs = (P("ctx", "head"),) * 4 + (P(None, "head"),) * 3
    return jax.shard_map(
        shards, mesh=mesh, in_specs=in_specs, out_specs=P("ctx", "head"), check_vma=False
    )
```
